32 devices in a mesh: seq: 16 (over z, y, x), mp: 2 (over core).
Axes of the slice: x: 2, y: 2, z: 4, core: 2. Of those that a mesh axis runs over, the one named last changes fastest.
Arguments:
- residual_in: bfloat16 [16384, 1024], P('seq'), may hold values from -6 to 6
- query_rows: bfloat16 [16384, 1024], P('seq', 'mp'), may hold values from -6 to 6
- key_rows: bfloat16 [16384, 1024], P('seq', 'mp'), may hold values from -6 to 6
- value_rows: bfloat16 [16384, 1024], P('seq', 'mp'), may hold values from -6 to 6
- rand_blocks: int32 [256, 16, 3], P(None, 'mp'), may hold values from 0 to 255, as said below
- global_blocks: int32 [2], replicated, may hold values from 0 to 255, as said below
- out_weight: bfloat16 [1024, 1024], P('mp'), may hold values from -0.1875 to 0.1875
- norm_gain: float32 [1024], replicated, may hold values from 0.25 to 1.75
- up_weight: bfloat16 [1024, 4096], P(None, 'mp'), may hold values from -0.1875 to 0.1875
- down_weight: bfloat16 [4096, 1024], P('mp'), may hold values from -0.09375 to 0.09375
Outputs:
- layer_out: bfloat16 [16384, 1024], P('seq', 'mp')
The draws below stay inside these ranges and needn't reach their ends.
Inputs may be any that keep to these rules, and one draw needn't show every extreme that they name: `rand_blocks`: each entry names a block of the same run of 16 consecutive groups of 16 blocks as its query block (groups counted from block 0). For every group of 16 query blocks, every set of 8 consecutive heads starting at a multiple of 8, and every group of its run, exactly 24 entries point into that group. `global_blocks`: the 2 entries differ; the last one is block 255.
All inputs are finite; a program needn't handle non-finite values.
Results may differ from the reference program's by a relative error of at most 0.006.
Values may be sent and summed in bfloat16 or wider, within the bound.
A program may use at most 256 MiB of HBM per device.

```python
import math
import jax
import jax.numpy as jnp
from jax import lax

D = 1024
H = 16
HD = 64
FF = 4096
BLK = 64
R = 3
GLOB = 2
GROUP = 16
QB_DEV = 16
TOK_DEV = 1024
NB = 256
TOKENS = 16384
HEADS_DEV = 8


def run_numbers():
    return jnp.arange(TOKENS, dtype=jnp.int32) // TOK_DEV


def draw_query_rows(key, part):
    drawn_draw = jnp.clip(jax.random.normal(jax.random.fold_in(key, 1), (TOKENS, D), jnp.float32), -4.5, 4.5)
    return drawn_draw.astype(jnp.bfloat16)


def draw_key_rows(key, part):
    drawn_draw = jnp.clip(jax.random.normal(jax.random.fold_in(key, 2), (TOKENS, D), jnp.float32), -4.5, 4.5)
    run_count = NB // QB_DEV
    run_shift = jax.random.uniform(jax.random.fold_in(key, 8), (run_count,), jnp.float32, -2.0, 2.0)
    direction = 2.0 * jax.random.randint(jax.random.fold_in(key, 9), (D,), 0, 2).astype(jnp.float32) - 1.0
    drawn_draw = jnp.clip(drawn_draw + run_shift[run_numbers()][:, None] * direction[None, :], -6.0, 6.0)
    return drawn_draw.astype(jnp.bfloat16)


def draw_value_rows(key, part):
    run_count = NB // QB_DEV
    drawn_draw = jnp.clip(jax.random.normal(jax.random.fold_in(key, 10), (TOKENS, D), jnp.float32), -4.5, 4.5)
    run_offset = jax.random.uniform(jax.random.fold_in(key, 11), (run_count, D), jnp.float32, -1.5, 1.5)
    return jnp.clip(drawn_draw + run_offset[run_numbers()], -6.0, 6.0).astype(jnp.bfloat16)


def draw_rand_blocks(key, part):
    shard_count = NB // QB_DEV
    halves = H // HEADS_DEV
    slot_count = QB_DEV * HEADS_DEV * R
    capacity = slot_count // GROUP
    key_list = jax.random.split(jax.random.fold_in(key, 3), shard_count * halves)
    slot_order = jax.vmap(lambda single_key: jax.random.permutation(single_key, slot_count))(key_list)
    offset_table = slot_order // capacity
    inner_block = jax.random.randint(jax.random.fold_in(key, 4), (shard_count * halves, slot_count), 0, QB_DEV)
    shard_ids = jnp.repeat(jnp.arange(shard_count, dtype=jnp.int32), halves)
    position = shard_ids % GROUP
    owner_shard = (shard_ids - position)[:, None] + (position[:, None] + offset_table) % GROUP
    block_table = owner_shard * QB_DEV + inner_block
    block_table = block_table.reshape(shard_count, halves, QB_DEV, HEADS_DEV, R).transpose(0, 2, 1, 3, 4).reshape(NB, H, R)
    return block_table.astype(jnp.int32)


def draw_global_blocks(key, part):
    first_block = jax.random.randint(jax.random.fold_in(key, 5), (), 0, NB - 1)
    return jnp.stack([first_block, jnp.array(NB - 1, dtype=jnp.int32)]).astype(jnp.int32)


def block_scale(rng, shape, shards, least, largest):
    loudness, own = 1.0, jax.random.fold_in(rng, 6)
    for axis_at, shards_of in shards:
        heights = jnp.exp(jax.random.uniform(jax.random.fold_in(own, axis_at), (shards_of,), jnp.float32, least / len(shards), largest / len(shards)))
        loudness = loudness * jnp.repeat(heights, shape[axis_at] // shards_of).reshape([-1 if axis == axis_at else 1 for axis in range(len(shape))])
    return loudness


def scatter_about(own_key, dims, width, reach, shards=(), kind=jnp.bfloat16):
    values = width * jax.random.normal(own_key, dims, jnp.float32)
    if shards:
        values = values * block_scale(own_key, dims, shards, -0.22, 0.18)
    return jnp.clip(values, -reach, reach).astype(kind)


def setup_inputs(seed: int = 0) -> dict:
    seeds = jax.random.split(jax.random.key(seed), 11)
    return {
        "residual_in": scatter_about(seeds[0], (TOKENS, D), 1.0, 6.0, ((0, 16),)),
        "query_rows": draw_query_rows(jax.random.fold_in(seeds[10], 71), 0),
        "key_rows": draw_key_rows(jax.random.fold_in(seeds[10], 71), 0),
        "value_rows": draw_value_rows(jax.random.fold_in(seeds[10], 71), 0),
        "rand_blocks": draw_rand_blocks(jax.random.fold_in(seeds[10], 71), 0),
        "global_blocks": draw_global_blocks(jax.random.fold_in(seeds[10], 71), 0),
        "out_weight": scatter_about(seeds[6], (D, D), D ** -0.5, 0.1875, ((0, 2),)),
        "norm_gain": jnp.clip(1.0 + 0.15 * jax.random.normal(seeds[7], (D,), jnp.float32), 0.25, 1.75),
        "up_weight": scatter_about(seeds[8], (D, FF), D ** -0.5, 0.1875, ((1, 2),)),
        "down_weight": scatter_about(seeds[9], (FF, D), FF ** -0.5, 0.09375, ((0, 2),)),
    }


def reference(residual_in, query_rows, key_rows, value_rows, rand_blocks, global_blocks, out_weight, norm_gain, up_weight, down_weight):
    score_scale = 1.0 / math.sqrt(HD)
    segments = NB // QB_DEV

    def heads_first(array):
        return array.reshape(NB, BLK, H, HD).transpose(2, 0, 1, 3)
    q_heads = heads_first(query_rows)
    k_heads = heads_first(key_rows)
    v_heads = heads_first(value_rows)
    rand_heads = rand_blocks.transpose(1, 0, 2).astype(jnp.int32)
    block_ids = jnp.arange(NB, dtype=jnp.int32)
    window = jnp.stack([(block_ids - 1) % NB, block_ids, (block_ids + 1) % NB], axis=1)
    global_cols = jnp.broadcast_to(global_blocks.astype(jnp.int32)[None, :], (NB, GLOB))
    always_on = jnp.ones((NB, 1), dtype=bool)
    valid_cols = jnp.concatenate([(block_ids >= 1)[:, None], always_on, (block_ids + 1 < NB)[:, None], jnp.ones((NB, R + GLOB), dtype=bool)], axis=1)

    def sparse_head(inputs):
        q_one, k_one, v_one, rand_one = inputs
        chosen = jnp.concatenate([window, rand_one, global_cols], axis=1)
        k_sel = k_one[chosen].astype(jnp.float32)
        v_sel = v_one[chosen].astype(jnp.float32)
        scores = jnp.einsum('nqd,njkd->nqjk', q_one.astype(jnp.float32), k_sel) * score_scale
        scores = jnp.where(valid_cols[:, None, :, None], scores, jnp.float32(-1e+30))
        row_peak = lax.optimization_barrier(jnp.max(scores, axis=(2, 3), keepdims=True))
        weights = jnp.exp(scores - row_peak)
        row_total = lax.optimization_barrier(jnp.sum(weights, axis=(2, 3)))
        rounded = lax.optimization_barrier(weights.astype(jnp.bfloat16)).astype(jnp.float32)
        mixed_sum = jnp.einsum('nqjk,njkd->nqd', rounded, v_sel)
        return mixed_sum / row_total[..., None]
    sparse_out = lax.map(sparse_head, (q_heads, k_heads, v_heads, rand_heads))

    def global_head(inputs):
        q_one, k_one, v_one = inputs
        global_q = q_one[global_blocks.astype(jnp.int32)].reshape(GLOB * BLK, HD).astype(jnp.float32)
        k_segs = k_one.reshape(segments, TOK_DEV, HD)
        v_segs = v_one.reshape(segments, TOK_DEV, HD)

        def fold_segment(state_now, segment):
            best, summed, accum = state_now
            k_seg, v_seg = segment
            scores = jnp.dot(global_q, k_seg.astype(jnp.float32).T) * score_scale
            seg_peak = lax.optimization_barrier(jnp.max(scores, axis=1))
            weights = jnp.exp(scores - seg_peak[:, None])
            seg_total = lax.optimization_barrier(jnp.sum(weights, axis=1))
            rounded = lax.optimization_barrier(weights.astype(jnp.bfloat16)).astype(jnp.float32)
            seg_acc = jnp.dot(rounded, v_seg.astype(jnp.float32))
            larger = jnp.maximum(best, seg_peak)
            factor_old = jnp.exp(best - larger)
            factor_new = jnp.exp(seg_peak - larger)
            return ((larger, summed * factor_old + seg_total * factor_new, accum * factor_old[:, None] + seg_acc * factor_new[:, None]), None)
        start_state = (jnp.full((GLOB * BLK,), -1e+30, dtype=jnp.float32), jnp.zeros((GLOB * BLK,), jnp.float32), jnp.zeros((GLOB * BLK, HD), jnp.float32))
        final_state, _ = lax.scan(fold_segment, start_state, (k_segs, v_segs))
        return (final_state[2] / final_state[1][:, None]).reshape(GLOB, BLK, HD)
    global_out = lax.map(global_head, (q_heads, k_heads, v_heads))
    merged = sparse_out.at[:, global_blocks.astype(jnp.int32)].set(global_out)
    attention = merged.transpose(1, 2, 0, 3).reshape(TOKENS, D).astype(jnp.bfloat16)
    projected = jnp.dot(attention, out_weight, preferred_element_type=jnp.float32)
    middle = (residual_in.astype(jnp.float32) + projected).astype(jnp.bfloat16)
    middle32 = middle.astype(jnp.float32)
    row_mean = lax.optimization_barrier(jnp.mean(middle32, axis=1, keepdims=True))
    centered = middle32 - row_mean
    row_var = lax.optimization_barrier(jnp.mean(centered * centered, axis=1, keepdims=True))
    normed = (centered * lax.rsqrt(row_var + 1e-05) * norm_gain).astype(jnp.bfloat16)
    hidden = jax.nn.gelu(jnp.dot(normed, up_weight, preferred_element_type=jnp.float32), approximate=True).astype(jnp.bfloat16)
    down_out = jnp.dot(hidden, down_weight, preferred_element_type=jnp.float32)
    return (middle32 + down_out).astype(jnp.bfloat16)
```

```python
import functools

import jax
import jax.numpy as jnp
from jax import lax
from jax.experimental import pallas as pl
from jax.experimental.pallas import tpu as pltpu
from jax.sharding import PartitionSpec as P

HD = 64
BLK = 64
R = 3
GLOB = 2
GROUP = 16
QB_DEV = 16
VMEM_LIMIT = 56 * 1024 * 1024
NT = (((1,), (1,)), ((), ()))


def half_mask(rows):
    return lax.broadcasted_iota(jnp.int32, (rows, 2 * HD), 1) < HD


def pack_kernel(index_ref, key_ref, value_ref, out_ref, tiles_ref):
    pairs = key_ref.shape[1] // (2 * HD)
    low = half_mask(BLK)

    def build(block, carry):
        rows = pl.ds(pl.multiple_of(block * BLK, BLK), BLK)
        for pair in range(pairs):
            cols = slice(pair * 2 * HD, (pair + 1) * 2 * HD)
            keys = key_ref[rows, cols].astype(jnp.float32)
            turned = pltpu.roll(value_ref[rows, cols].astype(jnp.float32), HD, 1)
            at = block * (2 * pairs) + 2 * pair
            tiles_ref[at] = jnp.where(low, keys, turned).astype(jnp.bfloat16)
            tiles_ref[at + 1] = jnp.where(low, turned, keys).astype(jnp.bfloat16)
        return carry

    lax.fori_loop(0, QB_DEV, build, 0)

    def pick(step, carry):
        for inner in range(8):
            slot = step * 8 + inner
            out_ref[slot] = tiles_ref[index_ref[slot]]
        return carry

    lax.fori_loop(0, out_ref.shape[0] // 8, pick, 0)


def pack(chosen, key_rows, value_rows):
    slots = chosen.shape[0]
    heads_here = key_rows.shape[1] // HD
    return pl.pallas_call(
        pack_kernel,
        out_shape=jax.ShapeDtypeStruct((slots, BLK, 2 * HD), jnp.bfloat16),
        in_specs=[
            pl.BlockSpec(memory_space=pltpu.SMEM),
            pl.BlockSpec(memory_space=pltpu.VMEM),
            pl.BlockSpec(memory_space=pltpu.VMEM),
        ],
        out_specs=pl.BlockSpec(memory_space=pltpu.VMEM),
        scratch_shapes=[pltpu.VMEM((QB_DEV * heads_here, BLK, 2 * HD), jnp.bfloat16)],
        compiler_params=pltpu.CompilerParams(vmem_limit_bytes=VMEM_LIMIT),
        name="pack",
    )(chosen, key_rows, value_rows)


def attend_kernel(
    slot_ref, first_ref, q_ref, k_ref, v_ref, gk_ref, gv_ref, rand_ref, out_ref
):
    block = pl.program_id(0)
    pairs = q_ref.shape[1] // (2 * HD)
    heads_here = 2 * pairs
    low = half_mask(BLK)
    rows = pl.ds(pl.multiple_of(block * BLK, BLK), 3 * BLK)
    cut_low = jnp.where((block == 0) & (first_ref[0] == 1), -1e30, 0.0)
    cut_high = jnp.where((block == QB_DEV - 1) & (first_ref[1] == 1), -1e30, 0.0)
    zeros = jnp.zeros((BLK, 2 * HD), jnp.bfloat16)
    for pair in range(pairs):
        cols = slice(pair * 2 * HD, (pair + 1) * 2 * HD)
        query = q_ref[:, cols] * jnp.bfloat16(HD**-0.5)
        q_even = jnp.where(low, query, zeros)
        q_odd = jnp.where(low, zeros, query)
        stacked = jnp.concatenate([q_even, q_odd], axis=0)
        spread = jnp.concatenate(
            [
                jnp.concatenate([q_even, zeros], axis=1),
                jnp.concatenate([zeros, q_odd], axis=1),
            ],
            axis=0,
        )
        random_tiles = []
        for r in range(R):
            at = (block * heads_here + 2 * pair) * R + r
            random_tiles.append(
                jnp.concatenate(
                    [rand_ref[slot_ref[at]], rand_ref[slot_ref[at + R]]], axis=1
                )
            )
        random_kv = jnp.concatenate(random_tiles, axis=0)
        keys = jnp.concatenate([k_ref[rows, cols], gk_ref[:, cols]], axis=0)
        values = jnp.concatenate([v_ref[rows, cols], gv_ref[:, cols]], axis=0)
        near = lax.dot_general(keys, stacked, NT, preferred_element_type=jnp.float32)
        far = lax.dot_general(random_kv, spread, NT, preferred_element_type=jnp.float32)
        near = jnp.concatenate(
            [near[:BLK] + cut_low, near[BLK : 2 * BLK], near[2 * BLK : 3 * BLK] + cut_high, near[3 * BLK :]],
            axis=0,
        )
        peak = jnp.maximum(
            jnp.max(near, axis=0, keepdims=True), jnp.max(far, axis=0, keepdims=True)
        )
        near = jnp.exp(near - peak)
        far = jnp.exp(far - peak)
        total = jnp.sum(near, axis=0, keepdims=True) + jnp.sum(far, axis=0, keepdims=True)
        contract = (((0,), (0,)), ((), ()))
        near_out = lax.dot_general(
            values, near.astype(jnp.bfloat16), contract, preferred_element_type=jnp.float32
        )
        far_out = lax.dot_general(
            random_kv, far.astype(jnp.bfloat16), contract, preferred_element_type=jnp.float32
        )
        even = near_out[:HD] + far_out[HD : 2 * HD]
        odd = near_out[HD:] + far_out[2 * HD : 3 * HD]
        lanes = lax.broadcasted_iota(jnp.int32, (HD, 2 * BLK), 1) < BLK
        both = jnp.concatenate([jnp.where(lanes, even, 0.0), jnp.where(lanes, 0.0, odd)], axis=0)
        both = (both / total).T
        out_ref[:, cols] = (both[:BLK] + both[BLK:]).astype(jnp.bfloat16)


def attend(slots, edges, query_rows, keys, values, global_k, global_v, received):
    tokens, width = query_rows.shape

    def whole(array):
        return pl.BlockSpec(array.shape, lambda i, *_: (0,) * array.ndim)

    return pl.pallas_call(
        attend_kernel,
        out_shape=jax.ShapeDtypeStruct((tokens, width), jnp.bfloat16),
        grid_spec=pltpu.PrefetchScalarGridSpec(
            num_scalar_prefetch=2,
            grid=(QB_DEV,),
            in_specs=[
                pl.BlockSpec((BLK, width), lambda i, *_: (i, 0)),
                whole(keys),
                whole(values),
                whole(global_k),
                whole(global_v),
                whole(received),
            ],
            out_specs=pl.BlockSpec((BLK, width), lambda i, *_: (i, 0)),
        ),
        compiler_params=pltpu.CompilerParams(vmem_limit_bytes=VMEM_LIMIT),
        name="attend",
    )(slots, edges, query_rows, keys, values, global_k, global_v, received)


def local(
    residual_in,
    query_rows,
    key_rows,
    value_rows,
    rand_blocks,
    global_blocks,
    out_weight,
    norm_gain,
    up_weight,
    down_weight,
):
    tok_rows, local_width = query_rows.shape
    heads_here = local_width // HD
    shard_count = lax.axis_size("seq")
    my_shard = lax.axis_index("seq")
    mp_index = lax.axis_index("mp")
    other = 1 - mp_index
    swap = [(0, 1), (1, 0)]
    score_scale = HD**-0.5
    position = my_shard % GROUP
    group_base = my_shard - position
    slot_count = QB_DEV * heads_here * R
    capacity = slot_count // GROUP

    wanted = lax.dynamic_slice_in_dim(
        rand_blocks, group_base * QB_DEV, GROUP * QB_DEV, 0
    ).reshape(GROUP, slot_count)
    counting = jnp.arange(slot_count, dtype=jnp.int32)
    earlier = (counting[:, None] < counting[None, :]).astype(jnp.bfloat16)
    slot_heads = counting // R % heads_here
    from_me = wanted // QB_DEV == my_shard
    my_requests = lax.dynamic_index_in_dim(wanted, position, 0, keepdims=False)
    owner = my_requests // QB_DEV - group_base
    by_owner = owner[None, :] == jnp.arange(GROUP, dtype=jnp.int32)[:, None]
    ranks = jnp.dot(
        jnp.concatenate([from_me, by_owner], axis=0).astype(jnp.bfloat16),
        earlier,
        preferred_element_type=jnp.float32,
    ).astype(jnp.int32)
    source = wanted % QB_DEV * heads_here + slot_heads[None, :]
    pick_table = from_me[:, None, :] & (
        ranks[:GROUP, None, :] == jnp.arange(capacity, dtype=jnp.int32)[None, :, None]
    )
    chosen = jnp.sum(jnp.where(pick_table, source[:, None, :], 0), axis=2)
    my_rank = jnp.sum(jnp.where(by_owner, ranks[GROUP:], 0), axis=0)
    slots = owner * capacity + my_rank

    sections = pack(chosen.reshape(slot_count), key_rows, value_rows)
    groups = [
        list(range(start, start + GROUP)) for start in range(0, shard_count, GROUP)
    ]
    received = lax.all_to_all(
        sections, "seq", 0, 0, axis_index_groups=groups, tiled=True
    )

    other_out = lax.ppermute(out_weight, "mp", swap)
    other_up = lax.ppermute(up_weight, "mp", swap)
    other_down = lax.ppermute(down_weight, "mp", swap)

    both = jnp.stack([key_rows, value_rows], axis=0)
    forward = [(i, i + 1) for i in range(shard_count - 1)]
    backward = [(i + 1, i) for i in range(shard_count - 1)]
    below = lax.ppermute(both[:, tok_rows - BLK :], "seq", forward)
    above = lax.ppermute(both[:, :BLK], "seq", backward)
    padded = jnp.concatenate([below, both, above], axis=1)

    packed = jnp.stack([query_rows, key_rows, value_rows], axis=0)
    contributions = []
    for which in range(GLOB):
        global_id = global_blocks[which]
        block_rows = lax.dynamic_slice_in_dim(packed, global_id % QB_DEV * BLK, BLK, 1)
        is_owner = global_id // QB_DEV == my_shard
        contributions.append(jnp.where(is_owner, block_rows, jnp.zeros_like(block_rows)))
    global_qkv = lax.psum(jnp.concatenate(contributions, axis=1), "seq")
    global_q = global_qkv[0].reshape(GLOB * BLK, heads_here, HD)
    global_k, global_v = global_qkv[1], global_qkv[2]

    key_heads = key_rows.reshape(tok_rows, heads_here, HD)
    value_heads = value_rows.reshape(tok_rows, heads_here, HD)
    global_scores = (
        jnp.einsum("qhd,thd->hqt", global_q, key_heads, preferred_element_type=jnp.float32)
        * score_scale
    )
    seg_peak = jnp.max(global_scores, axis=2)
    seg_weights = jnp.exp(global_scores - seg_peak[..., None])
    seg_total = jnp.sum(seg_weights, axis=2)
    seg_acc = jnp.einsum(
        "hqt,thd->hqd",
        seg_weights.astype(jnp.bfloat16),
        value_heads,
        preferred_element_type=jnp.float32,
    )
    stats = lax.all_gather(jnp.stack([seg_peak, seg_total], axis=0), "seq")
    top = jnp.max(stats[:, 0], axis=0)
    merged_total = jnp.sum(jnp.exp(stats[:, 0] - top) * stats[:, 1], axis=0)
    factor = jnp.exp(seg_peak - top) / merged_total
    global_out = lax.psum(seg_acc * factor[..., None], "seq")
    global_rows = (
        global_out.transpose(1, 0, 2).reshape(GLOB * BLK, local_width).astype(jnp.bfloat16)
    )

    edges = jnp.stack([my_shard == 0, my_shard == shard_count - 1]).astype(jnp.int32)
    attention = attend(
        slots, edges, query_rows, padded[0], padded[1], global_k, global_v, received
    )
    for which in range(GLOB):
        global_id = global_blocks[which]
        start_row = global_id % QB_DEV * BLK
        current = lax.dynamic_slice_in_dim(attention, start_row, BLK, 0)
        replacing = global_rows[which * BLK : (which + 1) * BLK]
        is_owner = global_id // QB_DEV == my_shard
        attention = lax.dynamic_update_slice_in_dim(
            attention, jnp.where(is_owner, replacing, current), start_row, 0
        )

    half_rows = tok_rows // 2
    half_width = residual_in.shape[1] // 2
    own_heads = lax.dynamic_slice_in_dim(attention, mp_index * half_rows, half_rows, 0)
    other_heads = lax.ppermute(
        lax.dynamic_slice_in_dim(attention, other * half_rows, half_rows, 0), "mp", swap
    )
    residual = lax.dynamic_slice_in_dim(residual_in, mp_index * half_rows, half_rows, 0)
    projected = jnp.dot(own_heads, out_weight, preferred_element_type=jnp.float32) + jnp.dot(
        other_heads, other_out, preferred_element_type=jnp.float32
    )
    middle = (residual.astype(jnp.float32) + projected).astype(jnp.bfloat16)
    middle32 = middle.astype(jnp.float32)
    row_mean = jnp.mean(middle32, axis=1, keepdims=True)
    centered = middle32 - row_mean
    row_var = jnp.mean(centered * centered, axis=1, keepdims=True)
    normed = (centered * lax.rsqrt(row_var + 1e-05) * norm_gain).astype(jnp.bfloat16)
    total = middle32
    for up, down in ((up_weight, down_weight), (other_up, other_down)):
        hidden = jax.nn.gelu(
            jnp.dot(normed, up, preferred_element_type=jnp.float32), approximate=True
        ).astype(jnp.bfloat16)
        total = total + jnp.dot(hidden, down, preferred_element_type=jnp.float32)
    result = total.astype(jnp.bfloat16)
    own_part = lax.dynamic_slice_in_dim(result, mp_index * half_width, half_width, 1)
    other_part = lax.ppermute(
        lax.dynamic_slice_in_dim(result, other * half_width, half_width, 1), "mp", swap
    )
    first = mp_index == 0
    return jnp.concatenate(
        [jnp.where(first, own_part, other_part), jnp.where(first, other_part, own_part)], axis=0
    )


def solution(mesh):
    placed = (
        P("seq", None),
        P("seq", "mp"),
        P("seq", "mp"),
        P("seq", "mp"),
        P(None, "mp", None),
        P(),
        P("mp", None),
        P(),
        P(None, "mp"),
        P("mp", None),
    )
    return jax.shard_map(
        local, mesh=mesh, in_specs=placed, out_specs=P("seq", "mp"), check_vma=False
    )
```

```python
import functools

import jax
import jax.numpy as jnp
from jax import lax
from jax.experimental import pallas as pl
from jax.experimental.pallas import tpu as pltpu
from jax.sharding import PartitionSpec as P

HD = 64
BLK = 64
R = 3
GLOB = 2
GROUP = 16
QB_DEV = 16
VMEM_LIMIT = 56 * 1024 * 1024
NT = (((1,), (1,)), ((), ()))
TT = (((0,), (0,)), ((), ()))


def half_mask(rows):
    return lax.broadcasted_iota(jnp.int32, (rows, 2 * HD), 1) < HD


def pack_kernel(index_ref, key_ref, value_ref, out_ref, tiles_ref):
    pairs = key_ref.shape[1] // (2 * HD)
    low = half_mask(BLK)

    def build(block, carry):
        rows = pl.ds(pl.multiple_of(block * BLK, BLK), BLK)
        for pair in range(pairs):
            cols = slice(pair * 2 * HD, (pair + 1) * 2 * HD)
            keys = key_ref[rows, cols].astype(jnp.float32)
            turned = pltpu.roll(value_ref[rows, cols].astype(jnp.float32), HD, 1)
            at = block * (2 * pairs) + 2 * pair
            tiles_ref[at] = jnp.where(low, keys, turned).astype(jnp.bfloat16)
            tiles_ref[at + 1] = jnp.where(low, turned, keys).astype(jnp.bfloat16)
        return carry

    lax.fori_loop(0, QB_DEV, build, 0)

    def pick(step, carry):
        for inner in range(8):
            slot = step * 8 + inner
            out_ref[slot] = tiles_ref[index_ref[slot]]
        return carry

    lax.fori_loop(0, out_ref.shape[0] // 8, pick, 0)


def pack(chosen, key_rows, value_rows):
    slots = chosen.shape[0]
    heads_here = key_rows.shape[1] // HD
    return pl.pallas_call(
        pack_kernel,
        out_shape=jax.ShapeDtypeStruct((slots, BLK, 2 * HD), jnp.bfloat16),
        in_specs=[
            pl.BlockSpec(memory_space=pltpu.SMEM),
            pl.BlockSpec(memory_space=pltpu.VMEM),
            pl.BlockSpec(memory_space=pltpu.VMEM),
        ],
        out_specs=pl.BlockSpec(memory_space=pltpu.VMEM),
        scratch_shapes=[pltpu.VMEM((QB_DEV * heads_here, BLK, 2 * HD), jnp.bfloat16)],
        compiler_params=pltpu.CompilerParams(vmem_limit_bytes=VMEM_LIMIT),
        name="pack",
    )(chosen, key_rows, value_rows)


def near_kernel(edge_ref, q_ref, k_ref, v_ref, gk_ref, gv_ref, acc_ref, stat_ref):
    block = pl.program_id(0)
    pairs = q_ref.shape[1] // (2 * HD)
    low = half_mask(BLK)
    rows = pl.ds(pl.multiple_of(block * BLK, BLK), 3 * BLK)
    cut_low = jnp.where((block == 0) & (edge_ref[0] == 1), -1e30, 0.0)
    cut_high = jnp.where((block == QB_DEV - 1) & (edge_ref[1] == 1), -1e30, 0.0)
    zeros = jnp.zeros((BLK, 2 * HD), jnp.bfloat16)
    lanes = lax.broadcasted_iota(jnp.int32, (HD, 2 * BLK), 1) < BLK
    for pair in range(pairs):
        cols = slice(pair * 2 * HD, (pair + 1) * 2 * HD)
        query = q_ref[:, cols] * jnp.bfloat16(HD**-0.5)
        stacked = jnp.concatenate(
            [jnp.where(low, query, zeros), jnp.where(low, zeros, query)], axis=0
        )
        keys = jnp.concatenate([k_ref[rows, cols], gk_ref[:, cols]], axis=0)
        values = jnp.concatenate([v_ref[rows, cols], gv_ref[:, cols]], axis=0)
        near = lax.dot_general(keys, stacked, NT, preferred_element_type=jnp.float32)
        near = jnp.concatenate(
            [
                near[:BLK] + cut_low,
                near[BLK : 2 * BLK],
                near[2 * BLK : 3 * BLK] + cut_high,
                near[3 * BLK :],
            ],
            axis=0,
        )
        peak = jnp.max(near, axis=0, keepdims=True)
        near = jnp.exp(near - peak)
        stat_ref[0, pair, 0:1, :] = peak
        stat_ref[0, pair, 1:2, :] = jnp.sum(near, axis=0, keepdims=True)
        out = lax.dot_general(
            values, near.astype(jnp.bfloat16), TT, preferred_element_type=jnp.float32
        )
        acc_ref[0, pair] = jnp.where(lanes, out[:HD], out[HD:])


def far_kernel(slot_ref, q_ref, rand_ref, acc_ref, stat_ref, out_ref):
    block = pl.program_id(0)
    pairs = q_ref.shape[1] // (2 * HD)
    heads_here = 2 * pairs
    low = half_mask(BLK)
    zeros = jnp.zeros((BLK, 2 * HD), jnp.bfloat16)
    lanes = lax.broadcasted_iota(jnp.int32, (HD, 2 * BLK), 1) < BLK
    for pair in range(pairs):
        cols = slice(pair * 2 * HD, (pair + 1) * 2 * HD)
        query = q_ref[:, cols] * jnp.bfloat16(HD**-0.5)
        spread = jnp.concatenate(
            [
                jnp.concatenate([jnp.where(low, query, zeros), zeros], axis=1),
                jnp.concatenate([zeros, jnp.where(low, zeros, query)], axis=1),
            ],
            axis=0,
        )
        tiles = []
        for r in range(R):
            at = (block * heads_here + 2 * pair) * R + r
            tiles.append(
                jnp.concatenate(
                    [rand_ref[slot_ref[at]], rand_ref[slot_ref[at + R]]], axis=1
                )
            )
        random_kv = jnp.concatenate(tiles, axis=0)
        far = lax.dot_general(random_kv, spread, NT, preferred_element_type=jnp.float32)
        near_peak = stat_ref[0, pair, 0:1, :]
        peak = jnp.maximum(near_peak, jnp.max(far, axis=0, keepdims=True))
        factor = jnp.exp(near_peak - peak)
        far = jnp.exp(far - peak)
        total = stat_ref[0, pair, 1:2, :] * factor + jnp.sum(far, axis=0, keepdims=True)
        out = lax.dot_general(
            random_kv, far.astype(jnp.bfloat16), TT, preferred_element_type=jnp.float32
        )
        merged = acc_ref[0, pair] * factor + jnp.where(
            lanes, out[HD : 2 * HD], out[2 * HD : 3 * HD]
        )
        merged = merged / total
        split = jnp.concatenate(
            [jnp.where(lanes, merged, 0.0), jnp.where(lanes, 0.0, merged)], axis=0
        ).T
        out_ref[:, cols] = (split[:BLK] + split[BLK:]).astype(jnp.bfloat16)


def whole(array):
    return pl.BlockSpec(array.shape, lambda i, *_: (0,) * array.ndim)


def by_block(*shape):
    return pl.BlockSpec((1,) + shape, lambda i, *_: (i,) + (0,) * len(shape))


def attend_near(edges, query_rows, keys, values, global_k, global_v):
    width = query_rows.shape[1]
    pairs = width // (2 * HD)
    return pl.pallas_call(
        near_kernel,
        out_shape=(
            jax.ShapeDtypeStruct((QB_DEV, pairs, HD, 2 * BLK), jnp.float32),
            jax.ShapeDtypeStruct((QB_DEV, pairs, 8, 2 * BLK), jnp.float32),
        ),
        grid_spec=pltpu.PrefetchScalarGridSpec(
            num_scalar_prefetch=1,
            grid=(QB_DEV,),
            in_specs=[
                pl.BlockSpec((BLK, width), lambda i, *_: (i, 0)),
                whole(keys),
                whole(values),
                whole(global_k),
                whole(global_v),
            ],
            out_specs=(by_block(pairs, HD, 2 * BLK), by_block(pairs, 8, 2 * BLK)),
        ),
        compiler_params=pltpu.CompilerParams(vmem_limit_bytes=VMEM_LIMIT),
        cost_estimate=pl.CostEstimate(
            flops=20_000_000_000, bytes_accessed=8_000_000, transcendentals=2_600_000
        ),
        name="attend_near",
    )(edges, query_rows, keys, values, global_k, global_v)


def attend_far(slots, query_rows, received, near_acc, near_stat):
    tokens, width = query_rows.shape
    pairs = width // (2 * HD)
    return pl.pallas_call(
        far_kernel,
        out_shape=jax.ShapeDtypeStruct((tokens, width), jnp.bfloat16),
        grid_spec=pltpu.PrefetchScalarGridSpec(
            num_scalar_prefetch=1,
            grid=(QB_DEV,),
            in_specs=[
                pl.BlockSpec((BLK, width), lambda i, *_: (i, 0)),
                whole(received),
                by_block(pairs, HD, 2 * BLK),
                by_block(pairs, 8, 2 * BLK),
            ],
            out_specs=pl.BlockSpec((BLK, width), lambda i, *_: (i, 0)),
        ),
        compiler_params=pltpu.CompilerParams(vmem_limit_bytes=VMEM_LIMIT),
        cost_estimate=pl.CostEstimate(
            flops=15_000_000_000, bytes_accessed=10_000_000, transcendentals=1_600_000
        ),
        name="attend_far",
    )(slots, query_rows, received, near_acc, near_stat)


def merge_parts(peak, total, accum):
    top = jnp.max(peak, axis=0)
    factor = jnp.exp(peak - top)
    return top, jnp.sum(total * factor, axis=0), jnp.sum(accum * factor[..., None], axis=0)


def local(
    residual_in,
    query_rows,
    key_rows,
    value_rows,
    rand_blocks,
    global_blocks,
    out_weight,
    norm_gain,
    up_weight,
    down_weight,
):
    tok_rows, local_width = query_rows.shape
    heads_here = local_width // HD
    shard_count = lax.axis_size("seq")
    my_shard = lax.axis_index("seq")
    mp_index = lax.axis_index("mp")
    other = 1 - mp_index
    swap = [(0, 1), (1, 0)]
    score_scale = HD**-0.5
    position = my_shard % GROUP
    group_base = my_shard - position
    slot_count = QB_DEV * heads_here * R
    capacity = slot_count // GROUP

    wanted = lax.dynamic_slice_in_dim(
        rand_blocks, group_base * QB_DEV, GROUP * QB_DEV, 0
    ).reshape(GROUP, slot_count)
    counting = jnp.arange(slot_count, dtype=jnp.int32)
    earlier = (counting[:, None] < counting[None, :]).astype(jnp.bfloat16)
    slot_heads = counting // R % heads_here
    from_me = wanted // QB_DEV == my_shard
    my_requests = lax.dynamic_index_in_dim(wanted, position, 0, keepdims=False)
    owner = my_requests // QB_DEV - group_base
    by_owner = owner[None, :] == jnp.arange(GROUP, dtype=jnp.int32)[:, None]
    ranks = jnp.dot(
        jnp.concatenate([from_me, by_owner], axis=0).astype(jnp.bfloat16),
        earlier,
        preferred_element_type=jnp.float32,
    ).astype(jnp.int32)
    source = wanted % QB_DEV * heads_here + slot_heads[None, :]
    pick_table = from_me[:, None, :] & (
        ranks[:GROUP, None, :] == jnp.arange(capacity, dtype=jnp.int32)[None, :, None]
    )
    chosen = jnp.sum(jnp.where(pick_table, source[:, None, :], 0), axis=2)
    my_rank = jnp.sum(jnp.where(by_owner, ranks[GROUP:], 0), axis=0)
    slots = owner * capacity + my_rank

    groups = [
        list(range(start, start + GROUP)) for start in range(0, shard_count, GROUP)
    ]
    both = jnp.stack([key_rows, value_rows], axis=0)
    forward = [(i, i + 1) for i in range(shard_count - 1)]
    backward = [(i + 1, i) for i in range(shard_count - 1)]
    below = lax.ppermute(both[:, tok_rows - BLK :], "seq", forward)
    above = lax.ppermute(both[:, :BLK], "seq", backward)

    packed = jnp.stack([query_rows, key_rows, value_rows], axis=0)
    contributions = []
    for which in range(GLOB):
        global_id = global_blocks[which]
        block_rows = lax.dynamic_slice_in_dim(packed, global_id % QB_DEV * BLK, BLK, 1)
        is_owner = global_id // QB_DEV == my_shard
        contributions.append(jnp.where(is_owner, block_rows, jnp.zeros_like(block_rows)))
    global_qkv = lax.psum(jnp.concatenate(contributions, axis=1), "seq")
    global_q = global_qkv[0].reshape(GLOB * BLK, heads_here, HD)
    global_k, global_v = global_qkv[1], global_qkv[2]

    key_heads = key_rows.reshape(tok_rows, heads_here, HD)
    value_heads = value_rows.reshape(tok_rows, heads_here, HD)
    global_scores = (
        jnp.einsum("qhd,thd->hqt", global_q, key_heads, preferred_element_type=jnp.float32)
        * score_scale
    )
    seg_peak = lax.reduce_precision(jnp.max(global_scores, axis=2), 8, 7)
    seg_weights = jnp.exp(global_scores - seg_peak[..., None])
    seg_total = jnp.sum(seg_weights, axis=2)
    seg_acc = jnp.einsum(
        "hqt,thd->hqd",
        seg_weights.astype(jnp.bfloat16),
        value_heads,
        preferred_element_type=jnp.float32,
    )
    total_high = lax.reduce_precision(seg_total, 8, 7)
    total_low = seg_total - total_high
    merge_rows = heads_here * GLOB * BLK // GROUP
    stats = jnp.stack([seg_peak, total_high, total_low], axis=-1)
    part = jnp.concatenate(
        [
            seg_acc,
            stats,
            jnp.zeros(seg_acc.shape[:2] + (HD - stats.shape[-1],), jnp.float32),
        ],
        axis=-1,
    ).astype(jnp.bfloat16)
    part = part.reshape(GROUP, 1, merge_rows, 2 * HD)

    tiles = pack(chosen.reshape(slot_count), key_rows, value_rows)
    tiles = tiles.reshape(GROUP, capacity, BLK, 2 * HD)
    tiles, part, below, above = lax.optimization_barrier((tiles, part, below, above))
    received, parts = (
        lax.all_to_all(block, "seq", 0, 0, axis_index_groups=groups, tiled=True)
        for block in (tiles, part)
    )
    received = received.reshape(slot_count, BLK, 2 * HD)

    other_out = lax.ppermute(out_weight, "mp", swap)
    other_up = lax.ppermute(up_weight, "mp", swap)
    other_down = lax.ppermute(down_weight, "mp", swap)

    edges = jnp.stack([my_shard == 0, my_shard == shard_count - 1]).astype(jnp.int32)
    padded = jnp.concatenate([below, both, above], axis=1)
    near_acc, near_stat = attend_near(
        edges, query_rows, padded[0], padded[1], global_k, global_v
    )

    parts = parts[:, 0].astype(jnp.float32)
    merged = merge_parts(
        parts[..., HD], parts[..., HD + 1] + parts[..., HD + 2], parts[..., :HD]
    )
    if shard_count > GROUP:
        across = [list(range(at, shard_count, GROUP)) for at in range(GROUP)]
        merged = merge_parts(
            *(lax.all_gather(one, "seq", axis_index_groups=across) for one in merged)
        )
    merged_rows = (merged[2] / merged[1][:, None]).astype(jnp.bfloat16)
    global_rows = lax.all_to_all(
        jnp.broadcast_to(merged_rows[None], (GROUP,) + merged_rows.shape),
        "seq",
        0,
        0,
        axis_index_groups=groups,
        tiled=True,
    )
    global_rows = (
        global_rows.reshape(heads_here, GLOB * BLK, HD)
        .transpose(1, 0, 2)
        .reshape(GLOB * BLK, local_width)
    )

    attention = attend_far(slots, query_rows, received, near_acc, near_stat)
    for which in range(GLOB):
        global_id = global_blocks[which]
        start_row = global_id % QB_DEV * BLK
        current = lax.dynamic_slice_in_dim(attention, start_row, BLK, 0)
        replacing = global_rows[which * BLK : (which + 1) * BLK]
        is_owner = global_id // QB_DEV == my_shard
        attention = lax.dynamic_update_slice_in_dim(
            attention, jnp.where(is_owner, replacing, current), start_row, 0
        )

    half_rows = tok_rows // 2
    half_width = residual_in.shape[1] // 2
    own_heads = lax.dynamic_slice_in_dim(attention, mp_index * half_rows, half_rows, 0)
    other_heads = lax.ppermute(
        lax.dynamic_slice_in_dim(attention, other * half_rows, half_rows, 0), "mp", swap
    )
    residual = lax.dynamic_slice_in_dim(residual_in, mp_index * half_rows, half_rows, 0)
    projected = jnp.dot(own_heads, out_weight, preferred_element_type=jnp.float32) + jnp.dot(
        other_heads, other_out, preferred_element_type=jnp.float32
    )
    middle = (residual.astype(jnp.float32) + projected).astype(jnp.bfloat16)
    middle32 = middle.astype(jnp.float32)
    row_mean = jnp.mean(middle32, axis=1, keepdims=True)
    centered = middle32 - row_mean
    row_var = jnp.mean(centered * centered, axis=1, keepdims=True)
    normed = (centered * lax.rsqrt(row_var + 1e-05) * norm_gain).astype(jnp.bfloat16)
    total = middle32
    for up, down in ((up_weight, down_weight), (other_up, other_down)):
        hidden = jax.nn.gelu(
            jnp.dot(normed, up, preferred_element_type=jnp.float32), approximate=True
        ).astype(jnp.bfloat16)
        total = total + jnp.dot(hidden, down, preferred_element_type=jnp.float32)
    result = total.astype(jnp.bfloat16)
    own_part = lax.dynamic_slice_in_dim(result, mp_index * half_width, half_width, 1)
    other_part = lax.ppermute(
        lax.dynamic_slice_in_dim(result, other * half_width, half_width, 1), "mp", swap
    )
    first = mp_index == 0
    return jnp.concatenate(
        [jnp.where(first, own_part, other_part), jnp.where(first, other_part, own_part)], axis=0
    )


def solution(mesh):
    placed = (
        P("seq", None),
        P("seq", "mp"),
        P("seq", "mp"),
        P("seq", "mp"),
        P(None, "mp", None),
        P(),
        P("mp", None),
        P(),
        P(None, "mp"),
        P("mp", None),
    )
    return jax.shard_map(
        local, mesh=mesh, in_specs=placed, out_specs=P("seq", "mp"), check_vma=False
    )
```

```python
import functools

import jax
import jax.numpy as jnp
from jax import lax
from jax.experimental import pallas as pl
from jax.experimental.pallas import tpu as pltpu
from jax.sharding import PartitionSpec as P

HD = 64
BLK = 64
R = 3
GLOB = 2
GROUP = 16
QB_DEV = 16
VMEM_LIMIT = 56 * 1024 * 1024
NT = (((1,), (1,)), ((), ()))
TT = (((0,), (0,)), ((), ()))


def half_mask(rows):
    return lax.broadcasted_iota(jnp.int32, (rows, 2 * HD), 1) < HD


def pack_kernel(index_ref, key_ref, value_ref, out_ref, tiles_ref):
    pairs = key_ref.shape[1] // (2 * HD)
    low = half_mask(BLK)

    def build(block, carry):
        rows = pl.ds(pl.multiple_of(block * BLK, BLK), BLK)
        for pair in range(pairs):
            cols = slice(pair * 2 * HD, (pair + 1) * 2 * HD)
            keys = key_ref[rows, cols].astype(jnp.float32)
            turned = pltpu.roll(value_ref[rows, cols].astype(jnp.float32), HD, 1)
            at = block * (2 * pairs) + 2 * pair
            tiles_ref[at] = jnp.where(low, keys, turned).astype(jnp.bfloat16)
            tiles_ref[at + 1] = jnp.where(low, turned, keys).astype(jnp.bfloat16)
        return carry

    lax.fori_loop(0, QB_DEV, build, 0)

    def pick(step, carry):
        for inner in range(8):
            slot = step * 8 + inner
            out_ref[slot] = tiles_ref[index_ref[slot]]
        return carry

    lax.fori_loop(0, out_ref.shape[0] // 8, pick, 0)


def pack(chosen, key_rows, value_rows):
    slots = chosen.shape[0]
    heads_here = key_rows.shape[1] // HD
    return pl.pallas_call(
        pack_kernel,
        out_shape=jax.ShapeDtypeStruct((slots, BLK, 2 * HD), jnp.bfloat16),
        in_specs=[
            pl.BlockSpec(memory_space=pltpu.SMEM),
            pl.BlockSpec(memory_space=pltpu.VMEM),
            pl.BlockSpec(memory_space=pltpu.VMEM),
        ],
        out_specs=pl.BlockSpec(memory_space=pltpu.VMEM),
        scratch_shapes=[pltpu.VMEM((QB_DEV * heads_here, BLK, 2 * HD), jnp.bfloat16)],
        compiler_params=pltpu.CompilerParams(vmem_limit_bytes=VMEM_LIMIT),
        name="pack",
    )(chosen, key_rows, value_rows)


def near_kernel(edge_ref, q_ref, k_ref, v_ref, gk_ref, gv_ref, acc_ref, stat_ref):
    block = pl.program_id(0)
    pairs = q_ref.shape[1] // (2 * HD)
    low = half_mask(BLK)
    rows = pl.ds(pl.multiple_of(block * BLK, BLK), 3 * BLK)
    cut_low = jnp.where((block == 0) & (edge_ref[0] == 1), -1e30, 0.0)
    cut_high = jnp.where((block == QB_DEV - 1) & (edge_ref[1] == 1), -1e30, 0.0)
    zeros = jnp.zeros((BLK, 2 * HD), jnp.bfloat16)
    lanes = lax.broadcasted_iota(jnp.int32, (HD, 2 * BLK), 1) < BLK
    for pair in range(pairs):
        cols = slice(pair * 2 * HD, (pair + 1) * 2 * HD)
        query = q_ref[:, cols] * jnp.bfloat16(HD**-0.5)
        stacked = jnp.concatenate(
            [jnp.where(low, query, zeros), jnp.where(low, zeros, query)], axis=0
        )
        keys = jnp.concatenate([k_ref[rows, cols], gk_ref[:, cols]], axis=0)
        values = jnp.concatenate([v_ref[rows, cols], gv_ref[:, cols]], axis=0)
        near = lax.dot_general(keys, stacked, NT, preferred_element_type=jnp.float32)
        near = jnp.concatenate(
            [
                near[:BLK] + cut_low,
                near[BLK : 2 * BLK],
                near[2 * BLK : 3 * BLK] + cut_high,
                near[3 * BLK :],
            ],
            axis=0,
        )
        peak = jnp.max(near, axis=0, keepdims=True)
        near = jnp.exp(near - peak)
        stat_ref[0, pair, 0:1, :] = peak
        stat_ref[0, pair, 1:2, :] = jnp.sum(near, axis=0, keepdims=True)
        out = lax.dot_general(
            values, near.astype(jnp.bfloat16), TT, preferred_element_type=jnp.float32
        )
        acc_ref[0, pair] = jnp.where(lanes, out[:HD], out[HD:])


def far_kernel(slot_ref, q_ref, rand_ref, acc_ref, stat_ref, out_ref):
    block = pl.program_id(0)
    pairs = q_ref.shape[1] // (2 * HD)
    heads_here = 2 * pairs
    low = half_mask(BLK)
    zeros = jnp.zeros((BLK, 2 * HD), jnp.bfloat16)
    lanes = lax.broadcasted_iota(jnp.int32, (HD, 2 * BLK), 1) < BLK
    for pair in range(pairs):
        cols = slice(pair * 2 * HD, (pair + 1) * 2 * HD)
        query = q_ref[:, cols] * jnp.bfloat16(HD**-0.5)
        spread = jnp.concatenate(
            [
                jnp.concatenate([jnp.where(low, query, zeros), zeros], axis=1),
                jnp.concatenate([zeros, jnp.where(low, zeros, query)], axis=1),
            ],
            axis=0,
        )
        tiles = []
        for r in range(R):
            at = (block * heads_here + 2 * pair) * R + r
            tiles.append(
                jnp.concatenate(
                    [rand_ref[slot_ref[at]], rand_ref[slot_ref[at + R]]], axis=1
                )
            )
        random_kv = jnp.concatenate(tiles, axis=0)
        far = lax.dot_general(random_kv, spread, NT, preferred_element_type=jnp.float32)
        near_peak = stat_ref[0, pair, 0:1, :]
        peak = jnp.maximum(near_peak, jnp.max(far, axis=0, keepdims=True))
        factor = jnp.exp(near_peak - peak)
        far = jnp.exp(far - peak)
        total = stat_ref[0, pair, 1:2, :] * factor + jnp.sum(far, axis=0, keepdims=True)
        out = lax.dot_general(
            random_kv, far.astype(jnp.bfloat16), TT, preferred_element_type=jnp.float32
        )
        merged = acc_ref[0, pair] * factor + jnp.where(
            lanes, out[HD : 2 * HD], out[2 * HD : 3 * HD]
        )
        merged = merged / total
        split = jnp.concatenate(
            [jnp.where(lanes, merged, 0.0), jnp.where(lanes, 0.0, merged)], axis=0
        ).T
        out_ref[:, cols] = (split[:BLK] + split[BLK:]).astype(jnp.bfloat16)


def whole(array):
    return pl.BlockSpec(array.shape, lambda i, *_: (0,) * array.ndim)


def by_block(*shape):
    return pl.BlockSpec((1,) + shape, lambda i, *_: (i,) + (0,) * len(shape))


def attend_near(edges, query_rows, keys, values, global_k, global_v):
    width = query_rows.shape[1]
    pairs = width // (2 * HD)
    return pl.pallas_call(
        near_kernel,
        out_shape=(
            jax.ShapeDtypeStruct((QB_DEV, pairs, HD, 2 * BLK), jnp.float32),
            jax.ShapeDtypeStruct((QB_DEV, pairs, 8, 2 * BLK), jnp.float32),
        ),
        grid_spec=pltpu.PrefetchScalarGridSpec(
            num_scalar_prefetch=1,
            grid=(QB_DEV,),
            in_specs=[
                pl.BlockSpec((BLK, width), lambda i, *_: (i, 0)),
                whole(keys),
                whole(values),
                whole(global_k),
                whole(global_v),
            ],
            out_specs=(by_block(pairs, HD, 2 * BLK), by_block(pairs, 8, 2 * BLK)),
        ),
        compiler_params=pltpu.CompilerParams(vmem_limit_bytes=VMEM_LIMIT),
        cost_estimate=pl.CostEstimate(
            flops=20_000_000_000, bytes_accessed=8_000_000, transcendentals=2_600_000
        ),
        name="attend_near",
    )(edges, query_rows, keys, values, global_k, global_v)


def attend_far(slots, query_rows, received, near_acc, near_stat):
    tokens, width = query_rows.shape
    pairs = width // (2 * HD)
    return pl.pallas_call(
        far_kernel,
        out_shape=jax.ShapeDtypeStruct((tokens, width), jnp.bfloat16),
        grid_spec=pltpu.PrefetchScalarGridSpec(
            num_scalar_prefetch=1,
            grid=(QB_DEV,),
            in_specs=[
                pl.BlockSpec((BLK, width), lambda i, *_: (i, 0)),
                whole(received),
                by_block(pairs, HD, 2 * BLK),
                by_block(pairs, 8, 2 * BLK),
            ],
            out_specs=pl.BlockSpec((BLK, width), lambda i, *_: (i, 0)),
        ),
        compiler_params=pltpu.CompilerParams(vmem_limit_bytes=VMEM_LIMIT),
        cost_estimate=pl.CostEstimate(
            flops=15_000_000_000, bytes_accessed=10_000_000, transcendentals=1_600_000
        ),
        name="attend_far",
    )(slots, query_rows, received, near_acc, near_stat)


def merge_parts(peak, total, accum):
    top = jnp.max(peak, axis=0)
    factor = jnp.exp(peak - top)
    return top, jnp.sum(total * factor, axis=0), jnp.sum(accum * factor[..., None], axis=0)


def local(
    residual_in,
    query_rows,
    key_rows,
    value_rows,
    rand_blocks,
    global_blocks,
    out_weight,
    norm_gain,
    up_weight,
    down_weight,
):
    tok_rows, local_width = query_rows.shape
    heads_here = local_width // HD
    shard_count = lax.axis_size("seq")
    my_shard = lax.axis_index("seq")
    mp_index = lax.axis_index("mp")
    other = 1 - mp_index
    swap = [(0, 1), (1, 0)]
    score_scale = HD**-0.5
    position = my_shard % GROUP
    group_base = my_shard - position
    slot_count = QB_DEV * heads_here * R
    capacity = slot_count // GROUP

    wanted = lax.dynamic_slice_in_dim(
        rand_blocks, group_base * QB_DEV, GROUP * QB_DEV, 0
    ).reshape(GROUP, slot_count)
    counting = jnp.arange(slot_count, dtype=jnp.int32)
    earlier = (counting[:, None] < counting[None, :]).astype(jnp.bfloat16)
    slot_heads = counting // R % heads_here
    from_me = wanted // QB_DEV == my_shard
    my_requests = lax.dynamic_index_in_dim(wanted, position, 0, keepdims=False)
    owner = my_requests // QB_DEV - group_base
    by_owner = owner[None, :] == jnp.arange(GROUP, dtype=jnp.int32)[:, None]
    ranks = jnp.dot(
        jnp.concatenate([from_me, by_owner], axis=0).astype(jnp.bfloat16),
        earlier,
        preferred_element_type=jnp.float32,
    ).astype(jnp.int32)
    source = wanted % QB_DEV * heads_here + slot_heads[None, :]
    pick_table = from_me[:, None, :] & (
        ranks[:GROUP, None, :] == jnp.arange(capacity, dtype=jnp.int32)[None, :, None]
    )
    chosen = jnp.sum(jnp.where(pick_table, source[:, None, :], 0), axis=2)
    my_rank = jnp.sum(jnp.where(by_owner, ranks[GROUP:], 0), axis=0)
    slots = owner * capacity + my_rank

    groups = [
        list(range(start, start + GROUP)) for start in range(0, shard_count, GROUP)
    ]
    both = jnp.stack([key_rows, value_rows], axis=0)
    forward = [(i, i + 1) for i in range(shard_count - 1)]
    backward = [(i + 1, i) for i in range(shard_count - 1)]
    below = lax.ppermute(both[:, tok_rows - BLK :], "seq", forward)
    above = lax.ppermute(both[:, :BLK], "seq", backward)

    packed = jnp.stack([query_rows, key_rows, value_rows], axis=0)
    contributions = []
    for which in range(GLOB):
        global_id = global_blocks[which]
        block_rows = lax.dynamic_slice_in_dim(packed, global_id % QB_DEV * BLK, BLK, 1)
        is_owner = global_id // QB_DEV == my_shard
        contributions.append(jnp.where(is_owner, block_rows, jnp.zeros_like(block_rows)))
    contributed = jnp.concatenate(contributions, axis=1)
    shares = contributed.reshape(shard_count, -1, local_width)
    shares = lax.all_to_all(shares, "seq", 0, 0, tiled=True)
    share = jnp.sum(shares.astype(jnp.float32), axis=0).astype(jnp.bfloat16)
    global_qkv = lax.all_to_all(
        jnp.broadcast_to(share[None], (shard_count,) + share.shape), "seq", 0, 0, tiled=True
    ).reshape(contributed.shape)
    global_q = global_qkv[0].reshape(GLOB * BLK, heads_here, HD)
    global_k, global_v = global_qkv[1], global_qkv[2]

    key_heads = key_rows.reshape(tok_rows, heads_here, HD)
    value_heads = value_rows.reshape(tok_rows, heads_here, HD)
    global_scores = (
        jnp.einsum("qhd,thd->hqt", global_q, key_heads, preferred_element_type=jnp.float32)
        * score_scale
    )
    seg_peak = lax.reduce_precision(jnp.max(global_scores, axis=2), 8, 7)
    seg_weights = jnp.exp(global_scores - seg_peak[..., None])
    seg_total = jnp.sum(seg_weights, axis=2)
    seg_acc = jnp.einsum(
        "hqt,thd->hqd",
        seg_weights.astype(jnp.bfloat16),
        value_heads,
        preferred_element_type=jnp.float32,
    )
    total_high = lax.reduce_precision(seg_total, 8, 7)
    total_low = seg_total - total_high
    merge_rows = heads_here * GLOB * BLK // GROUP
    stats = jnp.stack([seg_peak, total_high, total_low], axis=-1)
    part = jnp.concatenate(
        [
            seg_acc,
            stats,
            jnp.zeros(seg_acc.shape[:2] + (HD - stats.shape[-1],), jnp.float32),
        ],
        axis=-1,
    ).astype(jnp.bfloat16)
    part = part.reshape(GROUP, 1, merge_rows, 2 * HD)

    tiles = pack(chosen.reshape(slot_count), key_rows, value_rows)
    tiles = tiles.reshape(GROUP, capacity, BLK, 2 * HD)
    received, parts = (
        lax.all_to_all(block, "seq", 0, 0, axis_index_groups=groups, tiled=True)
        for block in (tiles, part)
    )
    received = received.reshape(slot_count, BLK, 2 * HD)

    other_out = lax.ppermute(out_weight, "mp", swap)
    other_up = lax.ppermute(up_weight, "mp", swap)
    other_down = lax.ppermute(down_weight, "mp", swap)

    edges = jnp.stack([my_shard == 0, my_shard == shard_count - 1]).astype(jnp.int32)
    padded = jnp.concatenate([below, both, above], axis=1)
    near_acc, near_stat = attend_near(
        edges, query_rows, padded[0], padded[1], global_k, global_v
    )

    parts = parts[:, 0].astype(jnp.float32)
    merged = merge_parts(
        parts[..., HD], parts[..., HD + 1] + parts[..., HD + 2], parts[..., :HD]
    )
    if shard_count > GROUP:
        across = [list(range(at, shard_count, GROUP)) for at in range(GROUP)]
        merged = merge_parts(
            *(lax.all_gather(one, "seq", axis_index_groups=across) for one in merged)
        )
    merged_rows = (merged[2] / merged[1][:, None]).astype(jnp.bfloat16)
    global_rows = lax.all_to_all(
        jnp.broadcast_to(merged_rows[None], (GROUP,) + merged_rows.shape),
        "seq",
        0,
        0,
        axis_index_groups=groups,
        tiled=True,
    )
    global_rows = (
        global_rows.reshape(heads_here, GLOB * BLK, HD)
        .transpose(1, 0, 2)
        .reshape(GLOB * BLK, local_width)
    )

    attention = attend_far(slots, query_rows, received, near_acc, near_stat)
    for which in range(GLOB):
        global_id = global_blocks[which]
        start_row = global_id % QB_DEV * BLK
        current = lax.dynamic_slice_in_dim(attention, start_row, BLK, 0)
        replacing = global_rows[which * BLK : (which + 1) * BLK]
        is_owner = global_id // QB_DEV == my_shard
        attention = lax.dynamic_update_slice_in_dim(
            attention, jnp.where(is_owner, replacing, current), start_row, 0
        )

    half_rows = tok_rows // 2
    half_width = residual_in.shape[1] // 2
    own_heads = lax.dynamic_slice_in_dim(attention, mp_index * half_rows, half_rows, 0)
    other_heads = lax.ppermute(
        lax.dynamic_slice_in_dim(attention, other * half_rows, half_rows, 0), "mp", swap
    )
    residual = lax.dynamic_slice_in_dim(residual_in, mp_index * half_rows, half_rows, 0)
    projected = jnp.dot(own_heads, out_weight, preferred_element_type=jnp.float32) + jnp.dot(
        other_heads, other_out, preferred_element_type=jnp.float32
    )
    middle = (residual.astype(jnp.float32) + projected).astype(jnp.bfloat16)
    middle32 = middle.astype(jnp.float32)
    row_mean = jnp.mean(middle32, axis=1, keepdims=True)
    centered = middle32 - row_mean
    row_var = jnp.mean(centered * centered, axis=1, keepdims=True)
    normed = (centered * lax.rsqrt(row_var + 1e-05) * norm_gain).astype(jnp.bfloat16)
    total = middle32
    for up, down in ((up_weight, down_weight), (other_up, other_down)):
        hidden = jax.nn.gelu(
            jnp.dot(normed, up, preferred_element_type=jnp.float32), approximate=True
        ).astype(jnp.bfloat16)
        total = total + jnp.dot(hidden, down, preferred_element_type=jnp.float32)
    result = total.astype(jnp.bfloat16)
    own_part = lax.dynamic_slice_in_dim(result, mp_index * half_width, half_width, 1)
    other_part = lax.ppermute(
        lax.dynamic_slice_in_dim(result, other * half_width, half_width, 1), "mp", swap
    )
    first = mp_index == 0
    return jnp.concatenate(
        [jnp.where(first, own_part, other_part), jnp.where(first, other_part, own_part)], axis=0
    )


def solution(mesh):
    placed = (
        P("seq", None),
        P("seq", "mp"),
        P("seq", "mp"),
        P("seq", "mp"),
        P(None, "mp", None),
        P(),
        P("mp", None),
        P(),
        P(None, "mp"),
        P("mp", None),
    )
    return jax.shard_map(
        local, mesh=mesh, in_specs=placed, out_specs=P("seq", "mp"), check_vma=False
    )
```

```python
import functools

import jax
import jax.numpy as jnp
from jax import lax
from jax.experimental import pallas as pl
from jax.experimental.pallas import tpu as pltpu
from jax.sharding import PartitionSpec as P

HD = 64
BLK = 64
R = 3
GLOB = 2
GROUP = 16
QB_DEV = 16
VMEM_LIMIT = 56 * 1024 * 1024
NT = (((1,), (1,)), ((), ()))
TT = (((0,), (0,)), ((), ()))


def half_mask(rows):
    return lax.broadcasted_iota(jnp.int32, (rows, 2 * HD), 1) < HD


def pack_kernel(index_ref, key_ref, value_ref, out_ref, tiles_ref):
    pairs = key_ref.shape[1] // (2 * HD)
    low = half_mask(BLK)

    def build(block, carry):
        rows = pl.ds(pl.multiple_of(block * BLK, BLK), BLK)
        for pair in range(pairs):
            cols = slice(pair * 2 * HD, (pair + 1) * 2 * HD)
            keys = key_ref[rows, cols].astype(jnp.float32)
            turned = pltpu.roll(value_ref[rows, cols].astype(jnp.float32), HD, 1)
            at = block * (2 * pairs) + 2 * pair
            tiles_ref[at] = jnp.where(low, keys, turned).astype(jnp.bfloat16)
            tiles_ref[at + 1] = jnp.where(low, turned, keys).astype(jnp.bfloat16)
        return carry

    lax.fori_loop(0, QB_DEV, build, 0)

    def pick(step, carry):
        for inner in range(8):
            slot = step * 8 + inner
            out_ref[slot] = tiles_ref[index_ref[slot]]
        return carry

    lax.fori_loop(0, out_ref.shape[0] // 8, pick, 0)


def pack(chosen, key_rows, value_rows):
    slots = chosen.shape[0]
    heads_here = key_rows.shape[1] // HD
    return pl.pallas_call(
        pack_kernel,
        out_shape=jax.ShapeDtypeStruct((slots, BLK, 2 * HD), jnp.bfloat16),
        in_specs=[
            pl.BlockSpec(memory_space=pltpu.SMEM),
            pl.BlockSpec(memory_space=pltpu.VMEM),
            pl.BlockSpec(memory_space=pltpu.VMEM),
        ],
        out_specs=pl.BlockSpec(memory_space=pltpu.VMEM),
        scratch_shapes=[pltpu.VMEM((QB_DEV * heads_here, BLK, 2 * HD), jnp.bfloat16)],
        compiler_params=pltpu.CompilerParams(vmem_limit_bytes=VMEM_LIMIT),
        name="pack",
    )(chosen, key_rows, value_rows)


def near_kernel(edge_ref, q_ref, k_ref, v_ref, gk_ref, gv_ref, acc_ref, stat_ref):
    block = pl.program_id(0)
    pairs = q_ref.shape[1] // (2 * HD)
    low = half_mask(BLK)
    rows = pl.ds(pl.multiple_of(block * BLK, BLK), 3 * BLK)
    cut_low = jnp.where((block == 0) & (edge_ref[0] == 1), -1e30, 0.0)
    cut_high = jnp.where((block == QB_DEV - 1) & (edge_ref[1] == 1), -1e30, 0.0)
    zeros = jnp.zeros((BLK, 2 * HD), jnp.bfloat16)
    lanes = lax.broadcasted_iota(jnp.int32, (HD, 2 * BLK), 1) < BLK
    for pair in range(pairs):
        cols = slice(pair * 2 * HD, (pair + 1) * 2 * HD)
        query = q_ref[:, cols] * jnp.bfloat16(HD**-0.5)
        stacked = jnp.concatenate(
            [jnp.where(low, query, zeros), jnp.where(low, zeros, query)], axis=0
        )
        keys = jnp.concatenate([k_ref[rows, cols], gk_ref[:, cols]], axis=0)
        values = jnp.concatenate([v_ref[rows, cols], gv_ref[:, cols]], axis=0)
        near = lax.dot_general(keys, stacked, NT, preferred_element_type=jnp.float32)
        near = jnp.concatenate(
            [
                near[:BLK] + cut_low,
                near[BLK : 2 * BLK],
                near[2 * BLK : 3 * BLK] + cut_high,
                near[3 * BLK :],
            ],
            axis=0,
        )
        peak = jnp.max(near, axis=0, keepdims=True)
        near = jnp.exp(near - peak)
        stat_ref[0, pair, 0:1, :] = peak
        stat_ref[0, pair, 1:2, :] = jnp.sum(near, axis=0, keepdims=True)
        out = lax.dot_general(
            values, near.astype(jnp.bfloat16), TT, preferred_element_type=jnp.float32
        )
        acc_ref[0, pair] = jnp.where(lanes, out[:HD], out[HD:])


def far_kernel(slot_ref, q_ref, rand_ref, acc_ref, stat_ref, out_ref):
    block = pl.program_id(0)
    pairs = q_ref.shape[1] // (2 * HD)
    heads_here = 2 * pairs
    low = half_mask(BLK)
    zeros = jnp.zeros((BLK, 2 * HD), jnp.bfloat16)
    lanes = lax.broadcasted_iota(jnp.int32, (HD, 2 * BLK), 1) < BLK
    for pair in range(pairs):
        cols = slice(pair * 2 * HD, (pair + 1) * 2 * HD)
        query = q_ref[:, cols] * jnp.bfloat16(HD**-0.5)
        spread = jnp.concatenate(
            [
                jnp.concatenate([jnp.where(low, query, zeros), zeros], axis=1),
                jnp.concatenate([zeros, jnp.where(low, zeros, query)], axis=1),
            ],
            axis=0,
        )
        tiles = []
        for r in range(R):
            at = (block * heads_here + 2 * pair) * R + r
            tiles.append(
                jnp.concatenate(
                    [rand_ref[slot_ref[at]], rand_ref[slot_ref[at + R]]], axis=1
                )
            )
        random_kv = jnp.concatenate(tiles, axis=0)
        far = lax.dot_general(random_kv, spread, NT, preferred_element_type=jnp.float32)
        near_peak = stat_ref[0, pair, 0:1, :]
        peak = jnp.maximum(near_peak, jnp.max(far, axis=0, keepdims=True))
        factor = jnp.exp(near_peak - peak)
        far = jnp.exp(far - peak)
        total = stat_ref[0, pair, 1:2, :] * factor + jnp.sum(far, axis=0, keepdims=True)
        out = lax.dot_general(
            random_kv, far.astype(jnp.bfloat16), TT, preferred_element_type=jnp.float32
        )
        merged = acc_ref[0, pair] * factor + jnp.where(
            lanes, out[HD : 2 * HD], out[2 * HD : 3 * HD]
        )
        merged = merged / total
        split = jnp.concatenate(
            [jnp.where(lanes, merged, 0.0), jnp.where(lanes, 0.0, merged)], axis=0
        ).T
        out_ref[:, cols] = (split[:BLK] + split[BLK:]).astype(jnp.bfloat16)


def whole(array):
    return pl.BlockSpec(array.shape, lambda i, *_: (0,) * array.ndim)


def by_block(*shape):
    return pl.BlockSpec((1,) + shape, lambda i, *_: (i,) + (0,) * len(shape))


def attend_near(edges, query_rows, keys, values, global_k, global_v):
    width = query_rows.shape[1]
    pairs = width // (2 * HD)
    return pl.pallas_call(
        near_kernel,
        out_shape=(
            jax.ShapeDtypeStruct((QB_DEV, pairs, HD, 2 * BLK), jnp.float32),
            jax.ShapeDtypeStruct((QB_DEV, pairs, 8, 2 * BLK), jnp.float32),
        ),
        grid_spec=pltpu.PrefetchScalarGridSpec(
            num_scalar_prefetch=1,
            grid=(QB_DEV,),
            in_specs=[
                pl.BlockSpec((BLK, width), lambda i, *_: (i, 0)),
                whole(keys),
                whole(values),
                whole(global_k),
                whole(global_v),
            ],
            out_specs=(by_block(pairs, HD, 2 * BLK), by_block(pairs, 8, 2 * BLK)),
        ),
        compiler_params=pltpu.CompilerParams(vmem_limit_bytes=VMEM_LIMIT),
        cost_estimate=pl.CostEstimate(
            flops=20_000_000_000, bytes_accessed=8_000_000, transcendentals=2_600_000
        ),
        name="attend_near",
    )(edges, query_rows, keys, values, global_k, global_v)


def attend_far(slots, query_rows, received, near_acc, near_stat):
    tokens, width = query_rows.shape
    pairs = width // (2 * HD)
    return pl.pallas_call(
        far_kernel,
        out_shape=jax.ShapeDtypeStruct((tokens, width), jnp.bfloat16),
        grid_spec=pltpu.PrefetchScalarGridSpec(
            num_scalar_prefetch=1,
            grid=(QB_DEV,),
            in_specs=[
                pl.BlockSpec((BLK, width), lambda i, *_: (i, 0)),
                whole(received),
                by_block(pairs, HD, 2 * BLK),
                by_block(pairs, 8, 2 * BLK),
            ],
            out_specs=pl.BlockSpec((BLK, width), lambda i, *_: (i, 0)),
        ),
        compiler_params=pltpu.CompilerParams(vmem_limit_bytes=VMEM_LIMIT),
        cost_estimate=pl.CostEstimate(
            flops=15_000_000_000, bytes_accessed=10_000_000, transcendentals=1_600_000
        ),
        name="attend_far",
    )(slots, query_rows, received, near_acc, near_stat)


def merge_parts(peak, total, accum):
    top = jnp.max(peak, axis=0)
    factor = jnp.exp(peak - top)
    return top, jnp.sum(total * factor, axis=0), jnp.sum(accum * factor[..., None], axis=0)


def local(
    residual_in,
    query_rows,
    key_rows,
    value_rows,
    rand_blocks,
    global_blocks,
    out_weight,
    norm_gain,
    up_weight,
    down_weight,
):
    tok_rows, local_width = query_rows.shape
    heads_here = local_width // HD
    shard_count = lax.axis_size("seq")
    my_shard = lax.axis_index("seq")
    mp_index = lax.axis_index("mp")
    other = 1 - mp_index
    swap = [(0, 1), (1, 0)]
    score_scale = HD**-0.5
    position = my_shard % GROUP
    group_base = my_shard - position
    slot_count = QB_DEV * heads_here * R
    capacity = slot_count // GROUP

    wanted = lax.dynamic_slice_in_dim(
        rand_blocks, group_base * QB_DEV, GROUP * QB_DEV, 0
    ).reshape(GROUP, slot_count)
    counting = jnp.arange(slot_count, dtype=jnp.int32)
    earlier = (counting[:, None] < counting[None, :]).astype(jnp.bfloat16)
    slot_heads = counting // R % heads_here
    from_me = wanted // QB_DEV == my_shard
    my_requests = lax.dynamic_index_in_dim(wanted, position, 0, keepdims=False)
    owner = my_requests // QB_DEV - group_base
    by_owner = owner[None, :] == jnp.arange(GROUP, dtype=jnp.int32)[:, None]
    ranks = jnp.dot(
        jnp.concatenate([from_me, by_owner], axis=0).astype(jnp.bfloat16),
        earlier,
        preferred_element_type=jnp.float32,
    ).astype(jnp.int32)
    source = wanted % QB_DEV * heads_here + slot_heads[None, :]
    pick_table = from_me[:, None, :] & (
        ranks[:GROUP, None, :] == jnp.arange(capacity, dtype=jnp.int32)[None, :, None]
    )
    chosen = jnp.sum(jnp.where(pick_table, source[:, None, :], 0), axis=2)
    my_rank = jnp.sum(jnp.where(by_owner, ranks[GROUP:], 0), axis=0)
    slots = owner * (capacity + 1) + my_rank

    groups = [
        list(range(start, start + GROUP)) for start in range(0, shard_count, GROUP)
    ]
    both = jnp.stack([key_rows, value_rows], axis=0)
    forward = [(i, i + 1) for i in range(shard_count - 1)]
    backward = [(i + 1, i) for i in range(shard_count - 1)]
    below = lax.ppermute(both[:, tok_rows - BLK :], "seq", forward)
    above = lax.ppermute(both[:, :BLK], "seq", backward)

    packed = jnp.stack([query_rows, key_rows, value_rows], axis=0)
    contributions = []
    for which in range(GLOB):
        global_id = global_blocks[which]
        block_rows = lax.dynamic_slice_in_dim(packed, global_id % QB_DEV * BLK, BLK, 1)
        is_owner = global_id // QB_DEV == my_shard
        contributions.append(jnp.where(is_owner, block_rows, jnp.zeros_like(block_rows)))
    contributed = jnp.concatenate(contributions, axis=1)
    shares = contributed.reshape(shard_count, -1, local_width)
    shares = lax.all_to_all(shares, "seq", 0, 0, tiled=True)
    share = jnp.sum(shares.astype(jnp.float32), axis=0).astype(jnp.bfloat16)
    global_qkv = lax.all_to_all(
        jnp.broadcast_to(share[None], (shard_count,) + share.shape), "seq", 0, 0, tiled=True
    ).reshape(contributed.shape)
    global_q = global_qkv[0].reshape(GLOB * BLK, heads_here, HD)
    global_k, global_v = global_qkv[1], global_qkv[2]

    key_heads = key_rows.reshape(tok_rows, heads_here, HD)
    value_heads = value_rows.reshape(tok_rows, heads_here, HD)
    global_scores = (
        jnp.einsum("qhd,thd->hqt", global_q, key_heads, preferred_element_type=jnp.float32)
        * score_scale
    )
    seg_peak = lax.reduce_precision(jnp.max(global_scores, axis=2), 8, 7)
    seg_weights = jnp.exp(global_scores - seg_peak[..., None])
    seg_total = jnp.sum(seg_weights, axis=2)
    seg_acc = jnp.einsum(
        "hqt,thd->hqd",
        seg_weights.astype(jnp.bfloat16),
        value_heads,
        preferred_element_type=jnp.float32,
    )
    total_high = lax.reduce_precision(seg_total, 8, 7)
    total_low = seg_total - total_high
    merge_rows = heads_here * GLOB * BLK // GROUP
    stats = jnp.stack([seg_peak, total_high, total_low], axis=-1)
    part = jnp.concatenate(
        [
            seg_acc,
            stats,
            jnp.zeros(seg_acc.shape[:2] + (HD - stats.shape[-1],), jnp.float32),
        ],
        axis=-1,
    ).astype(jnp.bfloat16)
    part = part.reshape(GROUP, 1, merge_rows, 2 * HD)

    chosen = jnp.pad(chosen, ((0, 0), (0, 1)))
    tiles = pack(chosen.reshape(GROUP * (capacity + 1)), key_rows, value_rows)
    tiles = tiles.reshape(GROUP, capacity + 1, BLK, 2 * HD)
    tiles = lax.dynamic_update_slice_in_dim(tiles, part, capacity, 1)
    tiles, below, above = lax.optimization_barrier((tiles, below, above))
    received = lax.all_to_all(
        tiles, "seq", 0, 0, axis_index_groups=groups, tiled=True
    )
    parts = received[:, capacity]
    received = received.reshape(GROUP * (capacity + 1), BLK, 2 * HD)

    other_out = lax.ppermute(out_weight, "mp", swap)
    other_up = lax.ppermute(up_weight, "mp", swap)
    other_down = lax.ppermute(down_weight, "mp", swap)

    edges = jnp.stack([my_shard == 0, my_shard == shard_count - 1]).astype(jnp.int32)
    padded = jnp.concatenate([below, both, above], axis=1)
    near_acc, near_stat = attend_near(
        edges, query_rows, padded[0], padded[1], global_k, global_v
    )

    parts = parts.astype(jnp.float32)
    merged = merge_parts(
        parts[..., HD], parts[..., HD + 1] + parts[..., HD + 2], parts[..., :HD]
    )
    if shard_count > GROUP:
        across = [list(range(at, shard_count, GROUP)) for at in range(GROUP)]
        merged = merge_parts(
            *(lax.all_gather(one, "seq", axis_index_groups=across) for one in merged)
        )
    merged_rows = (merged[2] / merged[1][:, None]).astype(jnp.bfloat16)
    global_rows = lax.all_to_all(
        jnp.broadcast_to(merged_rows[None], (GROUP,) + merged_rows.shape),
        "seq",
        0,
        0,
        axis_index_groups=groups,
        tiled=True,
    )
    global_rows = (
        global_rows.reshape(heads_here, GLOB * BLK, HD)
        .transpose(1, 0, 2)
        .reshape(GLOB * BLK, local_width)
    )

    attention = attend_far(slots, query_rows, received, near_acc, near_stat)
    for which in range(GLOB):
        global_id = global_blocks[which]
        start_row = global_id % QB_DEV * BLK
        current = lax.dynamic_slice_in_dim(attention, start_row, BLK, 0)
        replacing = global_rows[which * BLK : (which + 1) * BLK]
        is_owner = global_id // QB_DEV == my_shard
        attention = lax.dynamic_update_slice_in_dim(
            attention, jnp.where(is_owner, replacing, current), start_row, 0
        )

    half_rows = tok_rows // 2
    half_width = residual_in.shape[1] // 2
    own_heads = lax.dynamic_slice_in_dim(attention, mp_index * half_rows, half_rows, 0)
    other_heads = lax.ppermute(
        lax.dynamic_slice_in_dim(attention, other * half_rows, half_rows, 0), "mp", swap
    )
    residual = lax.dynamic_slice_in_dim(residual_in, mp_index * half_rows, half_rows, 0)
    projected = jnp.dot(own_heads, out_weight, preferred_element_type=jnp.float32) + jnp.dot(
        other_heads, other_out, preferred_element_type=jnp.float32
    )
    middle = (residual.astype(jnp.float32) + projected).astype(jnp.bfloat16)
    middle32 = middle.astype(jnp.float32)
    row_mean = jnp.mean(middle32, axis=1, keepdims=True)
    centered = middle32 - row_mean
    row_var = jnp.mean(centered * centered, axis=1, keepdims=True)
    normed = (centered * lax.rsqrt(row_var + 1e-05) * norm_gain).astype(jnp.bfloat16)
    total = middle32
    for up, down in ((up_weight, down_weight), (other_up, other_down)):
        hidden = jax.nn.gelu(
            jnp.dot(normed, up, preferred_element_type=jnp.float32), approximate=True
        ).astype(jnp.bfloat16)
        total = total + jnp.dot(hidden, down, preferred_element_type=jnp.float32)
    result = total.astype(jnp.bfloat16)
    own_part = lax.dynamic_slice_in_dim(result, mp_index * half_width, half_width, 1)
    other_part = lax.ppermute(
        lax.dynamic_slice_in_dim(result, other * half_width, half_width, 1), "mp", swap
    )
    first = mp_index == 0
    return jnp.concatenate(
        [jnp.where(first, own_part, other_part), jnp.where(first, other_part, own_part)], axis=0
    )


def solution(mesh):
    placed = (
        P("seq", None),
        P("seq", "mp"),
        P("seq", "mp"),
        P("seq", "mp"),
        P(None, "mp", None),
        P(),
        P("mp", None),
        P(),
        P(None, "mp"),
        P("mp", None),
    )
    return jax.shard_map(
        local, mesh=mesh, in_specs=placed, out_specs=P("seq", "mp"), check_vma=False
    )
```
